32 devices in a mesh: seq: 16 (over z, x, core), tp: 2 (over y).
Axes of the slice: x: 2, y: 2, z: 4, core: 2. Of those that a mesh axis runs over, the one named last changes fastest.
Arguments:
- noisy: bfloat16 [2, 6144, 1024], P(None, 'seq', 'tp'), may hold values from -6 to 6
- levels: int32 [2], replicated, may hold values from 0 to 999, as said below
- pairs: int32 [48, 4], P('seq'), may hold values from 0 to 47, as said below
- w_qkv: bfloat16 [3, 1024, 1024], P(None, None, 'tp'), may hold values from -4 to 4
- w_out: bfloat16 [1024, 1024], P('tp'), may hold values from -0.1875 to 0.1875
- w_up: bfloat16 [1024, 3072], P(None, 'tp'), may hold values from -0.1875 to 0.1875
- w_down: bfloat16 [3072, 1024], P('tp'), may hold values from -0.109375 to 0.109375
Outputs:
- denoised: bfloat16 [2, 6144, 1024], P(None, 'seq', 'tp')
The draws below stay inside these ranges and needn't reach their ends.
Inputs may be any that keep to these rules, and one draw needn't show every extreme that they name: For query block b and section s, pairs[b, s] lies in the group of 3 consecutive blocks numbered g XOR (48 * 128 // (384 * 2 ** (s + 1))), where g = b // 3; at each section the query blocks of one group name each block of that group once. The samples' levels differ from one another; one sample has level 999.
All inputs are finite; a program needn't handle non-finite values.
Results may differ from the reference program's by a relative error of at most 0.017.
Values may be sent and summed in bfloat16 or wider, within the bound.
A program may use at most 192 MiB of HBM per device.

```python
import math
import jax
import jax.numpy as jnp
from jax import lax

D = 1024
HEADS = 16
FF = 3072
BLOCK = 128
SECTIONS = 4
NLEV = 1000
SAMPLES = 2
TOK_DEV = 384
SEQLEN = 6144
NBLK = 48
N_SEQ = 16


def draw_levels(key, part):
    order = jax.random.permutation(jax.random.fold_in(key, 7), NLEV - 1)
    chosen = order[:SAMPLES].astype(jnp.int32)
    top_slot = jax.random.randint(jax.random.fold_in(key, 9), (), 0, SAMPLES, dtype=jnp.int32)
    slots = jnp.arange(SAMPLES, dtype=jnp.int32)
    return jnp.where(slots == top_slot, jnp.int32(NLEV - 1), chosen).astype(jnp.int32)


def draw_pairs(key, part):
    blocks_dev = TOK_DEV // BLOCK
    block_ids = jnp.arange(NBLK, dtype=jnp.int32)
    owners = block_ids // blocks_dev
    columns = []
    for section_idx in range(SECTIONS):
        shifts = jax.random.randint(jax.random.fold_in(key, 11 + section_idx), (N_SEQ,), 0, blocks_dev, dtype=jnp.int32)
        partner = jnp.bitwise_xor(owners, N_SEQ // 2 ** (section_idx + 1))
        offsets = (block_ids % blocks_dev + shifts[owners]) % blocks_dev
        columns.append(partner * blocks_dev + offsets)
    return jnp.stack(columns, axis=1).astype(jnp.int32)


def draw_w_qkv(key, part):
    base = jax.random.truncated_normal(jax.random.fold_in(key, 3), -4.0, 4.0, (3, D, D), jnp.float32)
    factors = jnp.array([2.0, 2.0, 1.0], jnp.float32) / math.sqrt(D)
    return (base * factors[:, None, None]).astype(jnp.bfloat16)


def level_of(key, shape, split, low, high):
    factor_of, own = 1.0, jax.random.fold_in(key, 6)
    for dim, shards_of in split:
        steps = jnp.exp(jax.random.uniform(jax.random.fold_in(own, dim), (shards_of,), jnp.float32, low / len(split), high / len(split)))
        factor_of = factor_of * jnp.repeat(steps, shape[dim] // shards_of).reshape([-1 if axis == dim else 1 for axis in range(len(shape))])
    return factor_of


def centred(key, shape, deviation, reach, split=(), kind=jnp.bfloat16):
    entries = jax.random.normal(key, shape, jnp.float32) * deviation
    if len(split) > 0:
        entries = level_of(key, shape, split, -0.22, 0.18) * entries
    return jnp.clip(entries, min=-reach, max=reach).astype(kind)


def setup_inputs(seed: int = 0) -> dict:
    splits = jax.random.split(jax.random.key(seed), 8)
    return {
        "noisy": centred(splits[0], (SAMPLES, SEQLEN, D), 1.0, 6.0, ((1, 16), (2, 2))),
        "levels": draw_levels(jax.random.fold_in(splits[7], 71), 0),
        "pairs": draw_pairs(jax.random.fold_in(splits[7], 71), 0),
        "w_qkv": draw_w_qkv(jax.random.fold_in(splits[7], 71), 0),
        "w_out": centred(splits[4], (D, D), D ** -0.5, 0.1875, ((0, 2),)),
        "w_up": centred(splits[5], (D, FF), D ** -0.5, 0.1875, ((1, 2),)),
        "w_down": centred(splits[6], (FF, D), FF ** -0.5, 0.109375, ((0, 2),)),
    }


def level_features(levels, model_width):
    half_count = model_width // 2
    index_row = jnp.arange(half_count, dtype=jnp.float32)
    freqs = jnp.exp(-math.log(10000.0) * index_row / half_count)
    angles = levels.astype(jnp.float32)[:, None] * freqs[None, :]
    return jnp.concatenate([jnp.sin(angles), jnp.cos(angles)], axis=1)

def rms_norm(values):
    return values * lax.rsqrt(lax.optimization_barrier(jnp.mean(values * values, axis=-1, keepdims=True)) + 1e-06)

def reference(noisy, levels, pairs, w_qkv, w_out, w_up, w_down):
    samples, seqlen, model_width = noisy.shape
    level_feat = level_features(levels, model_width)
    normed = (rms_norm(noisy.astype(jnp.float32)) + level_feat[:, None, :]).astype(jnp.bfloat16)
    flat = normed.reshape(samples * seqlen, model_width)
    projected = [jnp.dot(flat, w_qkv[which], preferred_element_type=jnp.float32).astype(jnp.bfloat16).reshape(samples, seqlen, model_width) for which in range(3)]
    queries, key_rows, value_rows = projected
    nblocks = seqlen // BLOCK
    blocks_dev = TOK_DEV // BLOCK
    head_dim = model_width // HEADS
    scale = 1.0 / math.sqrt(head_dim)
    zero_idx = jnp.int32(0)

    def denoise_block(item_idx):
        sample_idx = (item_idx // nblocks).astype(jnp.int32)
        block_idx = (item_idx % nblocks).astype(jnp.int32)
        start = (block_idx * BLOCK).astype(jnp.int32)
        group_start = (block_idx // blocks_dev * TOK_DEV).astype(jnp.int32)
        query_block = lax.dynamic_slice(queries, (sample_idx, start, zero_idx), (1, BLOCK, model_width))[0]
        key_parts = [lax.dynamic_slice(key_rows, (sample_idx, group_start, zero_idx), (1, TOK_DEV, model_width))[0]]
        value_parts = [lax.dynamic_slice(value_rows, (sample_idx, group_start, zero_idx), (1, TOK_DEV, model_width))[0]]
        for section_idx in range(SECTIONS):
            far_start = (pairs[block_idx, section_idx] * BLOCK).astype(jnp.int32)
            key_parts.append(lax.dynamic_slice(key_rows, (sample_idx, far_start, zero_idx), (1, BLOCK, model_width))[0])
            value_parts.append(lax.dynamic_slice(value_rows, (sample_idx, far_start, zero_idx), (1, BLOCK, model_width))[0])
        key_set = jnp.concatenate(key_parts, axis=0).astype(jnp.float32).reshape(-1, HEADS, head_dim)
        value_set = jnp.concatenate(value_parts, axis=0).astype(jnp.float32).reshape(-1, HEADS, head_dim)
        query_heads = query_block.astype(jnp.float32).reshape(BLOCK, HEADS, head_dim)
        scores = jnp.einsum('qhd,khd->hqk', query_heads, key_set) * scale
        probs = jax.nn.softmax(scores, axis=-1).astype(jnp.bfloat16)
        mixed = jnp.einsum('hqk,khd->qhd', probs.astype(jnp.float32), value_set).astype(jnp.bfloat16).reshape(BLOCK, model_width)
        inputs = lax.dynamic_slice(noisy, (sample_idx, start, zero_idx), (1, BLOCK, model_width))[0].astype(jnp.float32)
        middle = (inputs + jnp.dot(mixed, w_out, preferred_element_type=jnp.float32)).astype(jnp.bfloat16)
        inner = rms_norm(middle.astype(jnp.float32)).astype(jnp.bfloat16)
        hidden = jax.nn.gelu(jnp.dot(inner, w_up, preferred_element_type=jnp.float32), approximate=True).astype(jnp.bfloat16)
        return (middle.astype(jnp.float32) + jnp.dot(hidden, w_down, preferred_element_type=jnp.float32)).astype(jnp.bfloat16)
    items = jnp.arange(samples * nblocks, dtype=jnp.int32)
    result = lax.map(denoise_block, items)
    return result.reshape(samples, seqlen, model_width)
```

```python
import functools
import math

import jax
import jax.numpy as jnp
from jax import lax
from jax.experimental import pallas as pl
from jax.experimental.pallas import tpu as pltpu
from jax.sharding import PartitionSpec as P

HEADS = 16
BLOCK = 128
LANES = 128
RAW_SECTIONS = (0,)


def partner(x, axis, bit):
    return lax.ppermute(x, axis, [(i, i ^ 1 << bit) for i in range(lax.axis_size(axis))])


def both_halves(own, other, low):
    first = jnp.where(low, own, other)
    second = jnp.where(low, other, own)
    return jnp.concatenate([first, second], axis=-1)


def level_features(levels, model_width):
    half_count = model_width // 2
    index_row = jnp.arange(half_count, dtype=jnp.float32)
    freqs = jnp.exp(-math.log(10000.0) * index_row / half_count)
    angles = levels.astype(jnp.float32)[:, None] * freqs[None, :]
    return jnp.concatenate([jnp.sin(angles), jnp.cos(angles)], axis=1)


def rms_norm(values):
    return values * lax.rsqrt(jnp.mean(values * values, axis=-1, keepdims=True) + 1e-06)


def attention_kernel(sections, head_dim, offs, q_ref, near_ref, *rest):
    far_refs, out_ref = rest[:sections], rest[sections]
    rows = q_ref.shape[0]
    lane = lax.broadcasted_iota(jnp.int32, (BLOCK, LANES), 1)
    low = lane < head_dim
    scale = 1.0 / math.sqrt(head_dim)
    for b in range(rows // BLOCK):
        q = q_ref[b * BLOCK : (b + 1) * BLOCK, :].astype(jnp.float32) * scale
        q2 = jnp.concatenate([jnp.where(low, q, 0.0), jnp.where(low, 0.0, q)], axis=0)
        q2 = q2.astype(jnp.bfloat16)
        keys, values = [near_ref[0]], [near_ref[1]]
        for s in range(sections):
            at = pl.ds(pl.multiple_of(offs[b, s] * BLOCK, BLOCK), BLOCK)
            keys.append(far_refs[s][0, at, :])
            values.append(far_refs[s][1, at, :])
        keys = jnp.concatenate(keys, axis=0)
        values = jnp.concatenate(values, axis=0)
        scores = lax.dot_general(
            q2, keys, (((1,), (1,)), ((), ())), preferred_element_type=jnp.float32
        )
        top = jnp.max(scores, axis=-1, keepdims=True)
        probs = jnp.exp(scores - top)
        total = jnp.sum(probs, axis=-1, keepdims=True)
        mixed = jnp.dot(probs.astype(jnp.bfloat16), values, preferred_element_type=jnp.float32)
        mixed = mixed / total
        out_ref[b * BLOCK : (b + 1) * BLOCK, :] = jnp.where(
            low, mixed[:BLOCK], mixed[BLOCK:]
        ).astype(out_ref.dtype)


def attention(offsets, q, near, fars):
    rows, width = q.shape
    sections = len(fars)
    head_dim = 64
    key_count = rows + sections * BLOCK
    kv_spec = pl.BlockSpec((2, rows, LANES), lambda h, offs: (0, 0, h))
    row_spec = pl.BlockSpec((rows, LANES), lambda h, offs: (0, h))
    return pl.pallas_call(
        functools.partial(attention_kernel, sections, head_dim),
        out_shape=jax.ShapeDtypeStruct((rows, width), jnp.bfloat16),
        grid_spec=pltpu.PrefetchScalarGridSpec(
            num_scalar_prefetch=1,
            grid=(width // LANES,),
            in_specs=[row_spec] + [kv_spec] * (1 + sections),
            out_specs=row_spec,
        ),
        compiler_params=pltpu.CompilerParams(vmem_limit_bytes=24 * 2**20),
        cost_estimate=pl.CostEstimate(
            flops=8 * rows * key_count * width,
            bytes_accessed=2 * rows * width * (2 + 2 * (1 + sections)),
            transcendentals=rows * key_count * width // head_dim,
        ),
        name="attention",
    )(offsets, q, near, *fars)


def per_device(noisy, levels, pairs, w_qkv, w_out, w_up, w_down):
    samples, tok_rows, half_width = noisy.shape
    sections = pairs.shape[1]
    model_width = 2 * half_width
    blocks_dev = tok_rows // BLOCK
    axis_bits = lax.axis_size("seq").bit_length() - 1
    me = lax.axis_index("tp")
    low = me == 0
    bit_of = [axis_bits - 1 - s for s in range(sections)]
    offsets = (pairs % blocks_dev).astype(jnp.int32)
    level_feat = level_features(levels, model_width)
    w_q, w_kv = w_qkv[0], w_qkv[1:]

    own = [noisy[s] for s in range(samples)]
    other = [partner(x, "tp", 0) for x in own]
    raw = [{c: partner(x, "seq", bit_of[c]) for c in RAW_SECTIONS} for x in own]
    raw_other = [{c: partner(x, "tp", 0) for c, x in r.items()} for r in raw]
    w_out_other = partner(w_out, "tp", 0)

    def condition(full, s):
        return (rms_norm(full.astype(jnp.float32)) + level_feat[s]).astype(jnp.bfloat16)

    def keys_values(normed):
        return jnp.einsum(
            "td,cde->cte", normed, w_kv, preferred_element_type=jnp.float32
        ).astype(jnp.bfloat16)

    fulls, queries, nears, fars = [], [], [], []
    for s in range(samples):
        full = both_halves(own[s], other[s], low)
        normed = condition(full, s)
        near = keys_values(normed)
        far = {
            c: partner(near, "seq", bit_of[c]) for c in range(sections) if c not in RAW_SECTIONS
        }
        query = jnp.dot(normed, w_q, preferred_element_type=jnp.float32).astype(jnp.bfloat16)
        fulls.append(full)
        nears.append(near)
        fars.append(far)
        queries.append(query)
    for s in range(samples):
        for c in RAW_SECTIONS:
            far_full = both_halves(raw[s][c], raw_other[s][c], low)
            fars[s][c] = keys_values(condition(far_full, s))

    w_out_full = jnp.concatenate(
        [jnp.where(low, w_out, w_out_other), jnp.where(low, w_out_other, w_out)], axis=0
    )
    w_mine = lax.dynamic_slice_in_dim(w_down, me * half_width, half_width, 1)
    w_theirs = lax.dynamic_slice_in_dim(w_down, (1 - me) * half_width, half_width, 1)
    outs = []
    for s in range(samples):
        mixed = attention(offsets, queries[s], nears[s], [fars[s][c] for c in range(sections)])
        mixed_full = both_halves(mixed, partner(mixed, "tp", 0), low)
        attn = jnp.dot(mixed_full, w_out_full, preferred_element_type=jnp.float32)
        middle = (fulls[s].astype(jnp.float32) + attn).astype(jnp.bfloat16)
        inner = rms_norm(middle.astype(jnp.float32)).astype(jnp.bfloat16)
        hidden = jax.nn.gelu(
            jnp.dot(inner, w_up, preferred_element_type=jnp.float32), approximate=True
        ).astype(jnp.bfloat16)
        theirs = jnp.dot(hidden, w_theirs, preferred_element_type=jnp.float32)
        got = partner(theirs.astype(jnp.bfloat16), "tp", 0)
        mine = jnp.dot(hidden, w_mine, preferred_element_type=jnp.float32)
        middle_half = jnp.where(low, middle[:, :half_width], middle[:, half_width:])
        outs.append(
            (middle_half.astype(jnp.float32) + mine + got.astype(jnp.float32)).astype(jnp.bfloat16)
        )
    return jnp.stack(outs, axis=0)


def solution(mesh):
    in_specs = (
        P(None, "seq", "tp"),
        P(),
        P("seq", None),
        P(None, None, "tp"),
        P("tp", None),
        P(None, "tp"),
        P("tp", None),
    )
    out_specs = P(None, "seq", "tp")
    return jax.shard_map(
        per_device, mesh=mesh, in_specs=in_specs, out_specs=out_specs, check_vma=False
    )
```

```python
import functools
import math

import jax
import jax.numpy as jnp
from jax import lax
from jax.experimental import pallas as pl
from jax.experimental.pallas import tpu as pltpu
from jax.sharding import PartitionSpec as P

HEADS = 16
BLOCK = 128
LANES = 128


def partner(x, axis, bit):
    return lax.ppermute(x, axis, [(i, i ^ 1 << bit) for i in range(lax.axis_size(axis))])


def after(x, earlier):
    return lax.optimization_barrier((x, earlier))[0]


def join(own, other):
    return jnp.concatenate([own, other], axis=-1)


def halves_in_order(x, axis, keep):
    first, second = jnp.split(x, 2, axis=axis)
    return jnp.concatenate(
        [jnp.where(keep, first, second), jnp.where(keep, second, first)], axis=axis
    )


def level_features(levels, model_width):
    half_count = model_width // 2
    index_row = jnp.arange(half_count, dtype=jnp.float32)
    freqs = jnp.exp(-math.log(10000.0) * index_row / half_count)
    angles = levels.astype(jnp.float32)[:, None] * freqs[None, :]
    return jnp.concatenate([jnp.sin(angles), jnp.cos(angles)], axis=1)


def rms_norm(values):
    return values * lax.rsqrt(jnp.mean(values * values, axis=-1, keepdims=True) + 1e-06)


def attention_kernel(sections, head_dim, offs, q_ref, near_ref, *rest):
    far_refs, out_ref = rest[:sections], rest[sections]
    rows = q_ref.shape[0]
    lane = lax.broadcasted_iota(jnp.int32, (BLOCK, LANES), 1)
    low = lane < head_dim
    scale = 1.0 / math.sqrt(head_dim)
    for b in range(rows // BLOCK):
        q = q_ref[b * BLOCK : (b + 1) * BLOCK, :].astype(jnp.float32) * scale
        q2 = jnp.concatenate([jnp.where(low, q, 0.0), jnp.where(low, 0.0, q)], axis=0)
        q2 = q2.astype(jnp.bfloat16)
        keys, values = [near_ref[0]], [near_ref[1]]
        for s in range(sections):
            at = pl.ds(pl.multiple_of(offs[b, s] * BLOCK, BLOCK), BLOCK)
            keys.append(far_refs[s][0, at, :])
            values.append(far_refs[s][1, at, :])
        keys = jnp.concatenate(keys, axis=0)
        values = jnp.concatenate(values, axis=0)
        scores = lax.dot_general(
            q2, keys, (((1,), (1,)), ((), ())), preferred_element_type=jnp.float32
        )
        top = jnp.max(scores, axis=-1, keepdims=True)
        probs = jnp.exp(scores - top)
        total = jnp.sum(probs, axis=-1, keepdims=True)
        mixed = jnp.dot(probs.astype(jnp.bfloat16), values, preferred_element_type=jnp.float32)
        mixed = mixed / total
        out_ref[b * BLOCK : (b + 1) * BLOCK, :] = jnp.where(
            low, mixed[:BLOCK], mixed[BLOCK:]
        ).astype(out_ref.dtype)


def attention(offsets, q, near, fars):
    rows, width = q.shape
    sections = len(fars)
    head_dim = 64
    key_count = rows + sections * BLOCK
    kv_spec = pl.BlockSpec((2, rows, LANES), lambda h, offs: (0, 0, h))
    row_spec = pl.BlockSpec((rows, LANES), lambda h, offs: (0, h))
    return pl.pallas_call(
        functools.partial(attention_kernel, sections, head_dim),
        out_shape=jax.ShapeDtypeStruct((rows, width), jnp.bfloat16),
        grid_spec=pltpu.PrefetchScalarGridSpec(
            num_scalar_prefetch=1,
            grid=(width // LANES,),
            in_specs=[row_spec] + [kv_spec] * (1 + sections),
            out_specs=row_spec,
        ),
        compiler_params=pltpu.CompilerParams(vmem_limit_bytes=24 * 2**20),
        cost_estimate=pl.CostEstimate(
            flops=8 * rows * key_count * width,
            bytes_accessed=2 * rows * width * (2 + 2 * (1 + sections)),
            transcendentals=rows * key_count * width // head_dim,
        ),
        name="attention",
    )(offsets, q, near, *fars)


def per_device(noisy, levels, pairs, w_qkv, w_out, w_up, w_down):
    samples, tok_rows, half_width = noisy.shape
    sections = pairs.shape[1]
    model_width = 2 * half_width
    blocks_dev = tok_rows // BLOCK
    axis_bits = lax.axis_size("seq").bit_length() - 1
    me = lax.axis_index("tp")
    low = me == 0
    bit_of = [axis_bits - 1 - s for s in range(sections)]
    offsets = (pairs % blocks_dev).astype(jnp.int32)
    level_feat = halves_in_order(level_features(levels, model_width), 1, low)
    w_qkv, w_up, w_out_mine, w_out_sent = lax.optimization_barrier(
        (
            halves_in_order(w_qkv, 1, low),
            halves_in_order(w_up, 0, low),
            halves_in_order(w_out, 1, low),
            halves_in_order(w_out, 1, jnp.logical_not(low)),
        )
    )
    w_q, w_kv = w_qkv[0], w_qkv[1:]

    def condition(full, s):
        return (rms_norm(full.astype(jnp.float32)) + level_feat[s]).astype(jnp.bfloat16)

    def keys_values(normed):
        return jnp.einsum(
            "td,cde->cte", normed, w_kv, preferred_element_type=jnp.float32
        ).astype(jnp.bfloat16)

    own = [noisy[s] for s in range(samples)]
    fulls, queries, nears, fars, arrived = [], [], [], [], []
    other = raw = forwarded = None
    for s in range(samples):
        mine_tp = own[s] if other is None else after(own[s], other)
        mine_raw = own[s] if raw is None else after(own[s], raw)
        other = partner(mine_tp, "tp", 0)
        raw = partner(mine_raw, "seq", bit_of[0])
        full = join(own[s], other)
        normed = condition(full, s)
        near = keys_values(normed)
        far = {c: partner(near, "seq", bit_of[c]) for c in range(1, sections)}
        forwarded = partner(raw, "tp", 0)
        query = jnp.dot(normed, w_q, preferred_element_type=jnp.float32).astype(jnp.bfloat16)
        fulls.append(full)
        nears.append(near)
        fars.append(far)
        queries.append(query)
        arrived.append((raw, forwarded))
    first, second = jnp.split(after(w_out_sent, arrived[0][1]), 2, axis=0)
    even = lax.axis_index("seq") % 2 == 0
    fetched = partner(jnp.where(even, first, second), "tp", 0)
    swapped = partner(fetched, "seq", 0)
    w_out_other = [jnp.where(even, fetched, swapped), jnp.where(even, swapped, fetched)]

    w_out_full = jnp.concatenate([w_out_mine, *w_out_other], axis=0)
    w_mine = lax.dynamic_slice_in_dim(w_down, me * half_width, half_width, 1)
    w_theirs = lax.dynamic_slice_in_dim(w_down, (1 - me) * half_width, half_width, 1)
    outs = []
    mixed = None
    for s in range(samples):
        pair = arrived[s] if mixed is None else after(arrived[s], mixed)
        fars[s][0] = keys_values(condition(join(*pair), s))
        mixed = attention(offsets, queries[s], nears[s], [fars[s][c] for c in range(sections)])
        mixed_full = join(mixed, partner(mixed, "tp", 0))
        attn = jnp.dot(mixed_full, w_out_full, preferred_element_type=jnp.float32)
        middle = (fulls[s].astype(jnp.float32) + attn).astype(jnp.bfloat16)
        inner = rms_norm(middle.astype(jnp.float32)).astype(jnp.bfloat16)
        hidden = jax.nn.gelu(
            jnp.dot(inner, w_up, preferred_element_type=jnp.float32), approximate=True
        ).astype(jnp.bfloat16)
        theirs = jnp.dot(hidden, w_theirs, preferred_element_type=jnp.float32)
        got = partner(theirs.astype(jnp.bfloat16), "tp", 0)
        mine = jnp.dot(hidden, w_mine, preferred_element_type=jnp.float32)
        middle_half = middle[:, :half_width]
        outs.append(
            (middle_half.astype(jnp.float32) + mine + got.astype(jnp.float32)).astype(jnp.bfloat16)
        )
    return jnp.stack(outs, axis=0)


def solution(mesh):
    in_specs = (
        P(None, "seq", "tp"),
        P(),
        P("seq", None),
        P(None, None, "tp"),
        P("tp", None),
        P(None, "tp"),
        P("tp", None),
    )
    out_specs = P(None, "seq", "tp")
    return jax.shard_map(
        per_device, mesh=mesh, in_specs=in_specs, out_specs=out_specs, check_vma=False
    )
```

```python
import functools
import math

import jax
import jax.numpy as jnp
from jax import lax
from jax.experimental import pallas as pl
from jax.experimental.pallas import tpu as pltpu
from jax.sharding import PartitionSpec as P

HEADS = 16
BLOCK = 128
LANES = 128


def partner(x, axis, bit):
    return lax.ppermute(x, axis, [(i, i ^ 1 << bit) for i in range(lax.axis_size(axis))])


def after(x, earlier):
    return lax.optimization_barrier((x, earlier))[0]


def join(own, other):
    return jnp.concatenate([own, other], axis=-1)


def level_features(levels, model_width):
    half_count = model_width // 2
    index_row = jnp.arange(half_count, dtype=jnp.float32)
    freqs = jnp.exp(-math.log(10000.0) * index_row / half_count)
    angles = levels.astype(jnp.float32)[:, None] * freqs[None, :]
    return jnp.concatenate([jnp.sin(angles), jnp.cos(angles)], axis=1)


def attention_kernel(sections, head_dim, offs, q_ref, near_ref, *rest):
    far_refs, out_ref = rest[:sections], rest[sections]
    rows = q_ref.shape[0]
    lane = lax.broadcasted_iota(jnp.int32, (BLOCK, LANES), 1)
    low = lane < head_dim
    scale = 1.0 / math.sqrt(head_dim)
    for b in range(rows // BLOCK):
        q = q_ref[b * BLOCK : (b + 1) * BLOCK, :].astype(jnp.float32) * scale
        q2 = jnp.concatenate([jnp.where(low, q, 0.0), jnp.where(low, 0.0, q)], axis=0)
        q2 = q2.astype(jnp.bfloat16)
        keys, values = [near_ref[0]], [near_ref[1]]
        for s in range(sections):
            at = pl.ds(pl.multiple_of(offs[b, s] * BLOCK, BLOCK), BLOCK)
            keys.append(far_refs[s][0, at, :])
            values.append(far_refs[s][1, at, :])
        keys = jnp.concatenate(keys, axis=0)
        values = jnp.concatenate(values, axis=0)
        scores = lax.dot_general(
            q2, keys, (((1,), (1,)), ((), ())), preferred_element_type=jnp.float32
        )
        top = jnp.max(scores, axis=-1, keepdims=True)
        probs = jnp.exp(scores - top)
        total = jnp.sum(probs, axis=-1, keepdims=True)
        mixed = jnp.dot(probs.astype(jnp.bfloat16), values, preferred_element_type=jnp.float32)
        mixed = mixed / total
        out_ref[b * BLOCK : (b + 1) * BLOCK, :] = jnp.where(
            low, mixed[:BLOCK], mixed[BLOCK:]
        ).astype(out_ref.dtype)


def attention(offsets, q, near, fars):
    rows, width = q.shape
    sections = len(fars)
    head_dim = 64
    key_count = rows + sections * BLOCK
    kv_spec = pl.BlockSpec((2, rows, LANES), lambda h, offs: (0, 0, h))
    row_spec = pl.BlockSpec((rows, LANES), lambda h, offs: (0, h))
    return pl.pallas_call(
        functools.partial(attention_kernel, sections, head_dim),
        out_shape=jax.ShapeDtypeStruct((rows, width), jnp.bfloat16),
        grid_spec=pltpu.PrefetchScalarGridSpec(
            num_scalar_prefetch=1,
            grid=(width // LANES,),
            in_specs=[row_spec] + [kv_spec] * (1 + sections),
            out_specs=row_spec,
        ),
        compiler_params=pltpu.CompilerParams(vmem_limit_bytes=24 * 2**20),
        cost_estimate=pl.CostEstimate(
            flops=8 * rows * key_count * width,
            bytes_accessed=2 * rows * width * (2 + 2 * (1 + sections)),
            transcendentals=rows * key_count * width // head_dim,
        ),
        name="attention",
    )(offsets, q, near, *fars)


def per_device(noisy, levels, pairs, w_qkv, w_out, w_up, w_down):
    samples, tok_rows, half_width = noisy.shape
    sections = pairs.shape[1]
    model_width = 2 * half_width
    blocks_dev = tok_rows // BLOCK
    axis_bits = lax.axis_size("seq").bit_length() - 1
    me = lax.axis_index("tp")
    bit_of = [axis_bits - 1 - s for s in range(sections)]
    offsets = (pairs % blocks_dev).astype(jnp.int32)
    starts = (me * half_width, (1 - me) * half_width)
    level_feat = level_features(levels, model_width)
    level_halves = [lax.dynamic_slice_in_dim(level_feat, at, half_width, 1) for at in starts]
    w_q = [lax.dynamic_slice_in_dim(w_qkv[0], at, half_width, 0) for at in starts]
    w_kv = [lax.dynamic_slice_in_dim(w_qkv[1:], at, half_width, 1) for at in starts]
    w_in = [lax.dynamic_slice_in_dim(w_up, at, half_width, 0) for at in starts]

    def rms_halves(halves):
        halves = [x.astype(jnp.float32) for x in halves]
        squares = sum(jnp.sum(x * x, axis=-1, keepdims=True) for x in halves)
        factor = lax.rsqrt(squares / model_width + 1e-06)
        return [x * factor for x in halves]

    def condition(halves, s):
        return [
            (x + feat[s]).astype(jnp.bfloat16) for x, feat in zip(rms_halves(halves), level_halves)
        ]

    def products(halves, weights):
        return sum(
            jnp.dot(x, w, preferred_element_type=jnp.float32) for x, w in zip(halves, weights)
        )

    def keys_values(normed):
        return sum(
            jnp.einsum("td,cde->cte", x, w, preferred_element_type=jnp.float32)
            for x, w in zip(normed, w_kv)
        ).astype(jnp.bfloat16)

    own = [noisy[s] for s in range(samples)]
    fulls, queries, nears, fars, arrived = [], [], [], [], []
    raw = None
    for s in range(samples):
        mine_raw = own[s] if raw is None else after(own[s], raw)
        other = partner(own[s], "tp", 0)
        raw = partner(mine_raw, "seq", bit_of[0])
        full = (own[s], other)
        normed = condition(full, s)
        near = keys_values(normed)
        far = {c: partner(near, "seq", bit_of[c]) for c in range(1, sections)}
        forwarded = partner(raw, "tp", 0)
        query = products(normed, w_q).astype(jnp.bfloat16)
        fulls.append(full)
        nears.append(near)
        fars.append(far)
        queries.append(query)
        arrived.append((raw, forwarded))
    first, second = jnp.split(after(w_out, arrived[0][1]), 2, axis=0)
    even = lax.axis_index("seq") % 2 == 0
    fetched = partner(jnp.where(even, first, second), "tp", 0)
    swapped = partner(fetched, "seq", 0)
    w_out_other = [jnp.where(even, fetched, swapped), jnp.where(even, swapped, fetched)]

    w_out_full = jnp.concatenate([w_out, *w_out_other], axis=0)
    w_mixed = [lax.dynamic_slice_in_dim(w_out_full, at, half_width, 1) for at in starts]
    w_mine = lax.dynamic_slice_in_dim(w_down, me * half_width, half_width, 1)
    w_theirs = lax.dynamic_slice_in_dim(w_down, (1 - me) * half_width, half_width, 1)
    outs = []
    mixed = None
    for s in range(samples):
        pair = arrived[s] if mixed is None else after(arrived[s], mixed)
        fars[s][0] = keys_values(condition(pair, s))
        mixed = attention(offsets, queries[s], nears[s], [fars[s][c] for c in range(sections)])
        received = partner(mixed, "tp", 0)
        if s > 0:
            received = after(received, theirs)
        mixed_full = join(mixed, received)
        middle = [
            (x.astype(jnp.float32) + jnp.dot(mixed_full, w, preferred_element_type=jnp.float32))
            .astype(jnp.bfloat16)
            for x, w in zip(fulls[s], w_mixed)
        ]
        inner = [x.astype(jnp.bfloat16) for x in rms_halves(middle)]
        hidden = jax.nn.gelu(products(inner, w_in), approximate=True).astype(jnp.bfloat16)
        theirs = jnp.dot(hidden, w_theirs, preferred_element_type=jnp.float32)
        got = partner(theirs.astype(jnp.bfloat16), "tp", 0)
        mine = jnp.dot(hidden, w_mine, preferred_element_type=jnp.float32)
        outs.append(
            (middle[0].astype(jnp.float32) + mine + got.astype(jnp.float32)).astype(jnp.bfloat16)
        )
    return jnp.stack(outs, axis=0)


def solution(mesh):
    in_specs = (
        P(None, "seq", "tp"),
        P(),
        P("seq", None),
        P(None, None, "tp"),
        P("tp", None),
        P(None, "tp"),
        P("tp", None),
    )
    out_specs = P(None, "seq", "tp")
    return jax.shard_map(
        per_device, mesh=mesh, in_specs=in_specs, out_specs=out_specs, check_vma=False
    )
```
